256 devices in a mesh: ctx: 64 (over z, y, core), head: 4 (over x).
Axes of the slice: x: 4, y: 4, z: 8, core: 2. Of those that a mesh axis runs over, the one named last changes fastest.
Arguments:
- queries: bfloat16 [24576, 4096], P(('ctx', 'head')), may hold values from -7 to 7
- keys: bfloat16 [24576, 1024], P(('ctx', 'head')), may hold values from -7 to 7
- values: bfloat16 [24576, 1024], P(('ctx', 'head')), may hold values from -6 to 6
- out_grad: bfloat16 [24576, 4096], P(('ctx', 'head')), may hold values from -6 to 6
- doc_ids: int32 [24576], P('ctx'), may hold values from 0 to 63, never falling along the last dimension, each value on 1 to 1152 neighbouring positions
Outputs:
- attention_out: bfloat16 [24576, 4096], P(('ctx', 'head'))
- query_grad: bfloat16 [24576, 4096], P(('ctx', 'head'))
- key_grad: bfloat16 [24576, 1024], P(('ctx', 'head'))
- value_grad: bfloat16 [24576, 1024], P(('ctx', 'head'))
The draws below stay inside these ranges and needn't reach their ends.
Inputs may be any that keep to these rules, and one draw needn't show every extreme that they name: `doc_ids`: never falls along the batch; every document has 1 to 1152 tokens, and one has exactly 1152.
All inputs are finite; a program needn't handle non-finite values.
Results may differ from the reference program's by a relative error of at most 0.025.
Values may be sent and summed in bfloat16 or wider, within the bound.
No kernel may reach another device: no remote copies, remote signals or barrier semaphores. Data moves between devices by JAX's collectives and lax.ppermute only.
A program may use at most 128 MiB of HBM per device.

```python
import math
import jax
import jax.numpy as jnp
import numpy as np
from jax import lax

QHEADS = 32
KVHEADS = 8
HDIM = 128
ROWS = 384
REACH = 3
TOKENS = 24576
DOCS = 64


def draw_queries(key, part):
    key = jax.random.fold_in(key, 1)
    drawn = jnp.clip(jax.random.normal(key, (TOKENS, QHEADS, HDIM), jnp.float32), -4.0, 4.0)
    return drawn.reshape(TOKENS, QHEADS * HDIM).astype(jnp.bfloat16)


def draw_keys(key, part):
    key = jax.random.fold_in(key, 2)
    drawn = jnp.clip(jax.random.normal(key, (TOKENS, KVHEADS, HDIM), jnp.float32), -4.0, 4.0)
    return drawn.reshape(TOKENS, KVHEADS * HDIM).astype(jnp.bfloat16)


def block_scale(key, dims, split, low, largest):
    gain, own = 1.0, jax.random.fold_in(key, 6)
    for position, blocks in split:
        steps = jnp.exp(jax.random.uniform(jax.random.fold_in(own, position), (blocks,), jnp.float32, low / len(split), largest / len(split)))
        gain = gain * jnp.repeat(steps, dims[position] // blocks).reshape([-1 if axis == position else 1 for axis in range(len(dims))])
    return gain


def profile(amount, total, reach, lean):
    loads = [(1 << 20) // math.isqrt(rank ** lean) + 1 for rank in range(2, amount + 1)]
    rest, given = total - reach - (amount - 1), [1] * (amount - 1)
    while rest > 0:
        free = [i for i in range(amount - 1) if given[i] < reach]
        whole, remaining = sum([loads[i] for i in free]), rest
        for i in free:
            extra = min(reach - given[i], max(1, remaining * loads[i] // whole), rest)
            given[i] = given[i] + extra
            rest = rest - extra
    return np.array([reach] + given)


def uneven_parts(stream_key, amount, total, bound, lean):
    if amount == 2:
        one = jax.random.randint(stream_key, (), max(1, total - bound), min(bound, total - 1) + 1)
        return jnp.stack([one, total - one])
    tallies = jnp.asarray(profile(amount, total, bound, lean), jnp.int32)
    twos = (amount - 1) // 2
    giver, sink = tallies[1:1 + 2 * twos:2], tallies[2:2 + 2 * twos:2]
    slack = jnp.minimum(giver - 1, bound - sink)
    passed = jax.random.randint(jax.random.fold_in(stream_key, 1), (twos,), 0, 1 << 20) % (slack + 1)
    tallies = tallies.at[1:1 + 2 * twos:2].set(giver - passed).at[2:2 + 2 * twos:2].set(sink + passed)
    return tallies[jax.random.permutation(jax.random.fold_in(stream_key, 2), amount)]


def normal_values(key, dims, spread, most, pieces=(), kind=jnp.bfloat16):
    factor_of = block_scale(key, dims, pieces, -0.22, 0.18) if pieces else 1.0
    result = jax.random.normal(key, dims, jnp.float32) * spread * factor_of
    return jnp.minimum(jnp.maximum(result, -most), most).astype(kind)


def setup_inputs(seed: int = 0) -> dict:
    key_of = jax.random.split(jax.random.key(seed), 6)
    queries = draw_queries(jax.random.fold_in(key_of[5], 71), 0)
    keys = draw_keys(jax.random.fold_in(key_of[5], 71), 0)
    values = normal_values(key_of[2], (TOKENS, KVHEADS * HDIM), 1.0, 6.0, ((0, 256),))
    out_grad = normal_values(key_of[3], (TOKENS, QHEADS * HDIM), 1.0, 6.0, ((0, 256),))
    doc_ids = jnp.searchsorted(jnp.cumsum(uneven_parts(key_of[4], DOCS, TOKENS, REACH * ROWS, 1)), jnp.arange(TOKENS), side="right").astype(jnp.int32)
    return dict(queries=queries, keys=keys, values=values, out_grad=out_grad, doc_ids=doc_ids)


masked_score = -1.0e30


def reference(queries, keys, values, out_grad, doc_ids):
    repeat = QHEADS // KVHEADS
    score_scale = HDIM ** -0.5
    reach_rows = REACH * ROWS
    window = reach_rows + ROWS
    query_all = queries.reshape(TOKENS, KVHEADS, repeat, HDIM).astype(jnp.float32)
    grad_all = out_grad.reshape(TOKENS, KVHEADS, repeat, HDIM).astype(jnp.float32)
    key_pad = jnp.concatenate([jnp.zeros((reach_rows, KVHEADS, HDIM), jnp.float32), keys.reshape(TOKENS, KVHEADS, HDIM).astype(jnp.float32)], 0)
    value_pad = jnp.concatenate([jnp.zeros((reach_rows, KVHEADS, HDIM), jnp.float32), values.reshape(TOKENS, KVHEADS, HDIM).astype(jnp.float32)], 0)
    doc_pad = jnp.concatenate([jnp.full((reach_rows,), -1, jnp.int32), doc_ids.astype(jnp.int32)])
    offsets = jnp.arange(ROWS, dtype=jnp.int32)
    key_offsets = jnp.arange(window, dtype=jnp.int32)

    def one_block(grads_carry, block_index):
        key_acc, value_acc = grads_carry
        first_row = (block_index * ROWS).astype(jnp.int32)
        query_block = lax.dynamic_slice_in_dim(query_all, first_row, ROWS, 0)
        grad_block = lax.dynamic_slice_in_dim(grad_all, first_row, ROWS, 0)
        doc_block = lax.dynamic_slice_in_dim(doc_ids.astype(jnp.int32), first_row, ROWS, 0)
        key_block = lax.dynamic_slice_in_dim(key_pad, first_row, window, 0)
        value_block = lax.dynamic_slice_in_dim(value_pad, first_row, window, 0)
        doc_keys = lax.dynamic_slice_in_dim(doc_pad, first_row, window, 0)
        allowed = (doc_block[:, None] == doc_keys[None, :]) & (key_offsets[None, :] <= offsets[:, None] + reach_rows)
        scores = jnp.einsum("qgrd,kgd->grqk", query_block, key_block) * score_scale
        scores = jnp.where(allowed, scores, masked_score)
        highest = jnp.max(scores, -1)
        log_total = highest + jnp.log(jnp.sum(jnp.exp(scores - highest[..., None]), -1))
        weights_full = jnp.where(allowed, jnp.exp(scores - log_total[..., None]), 0.0)
        probs_low = lax.optimization_barrier(weights_full.astype(jnp.bfloat16)).astype(jnp.float32)
        out_block = jnp.einsum("grqk,kgd->qgrd", probs_low, value_block).astype(jnp.bfloat16)
        row_dots = jnp.transpose(jnp.sum(grad_block * out_block.astype(jnp.float32), -1), (1, 2, 0))
        grad_probs = jnp.einsum("qgrd,kgd->grqk", grad_block, value_block)
        grad_scores = weights_full * (grad_probs - row_dots[..., None])
        grad_scores = lax.optimization_barrier(grad_scores.astype(jnp.bfloat16)).astype(jnp.float32)
        query_block_grad = (jnp.einsum("grqk,kgd->qgrd", grad_scores, key_block) * score_scale).astype(jnp.bfloat16)
        key_term = jnp.einsum("grqk,qgrd->kgd", grad_scores, query_block) * score_scale
        value_term = jnp.einsum("grqk,qgrd->kgd", probs_low, grad_block)
        key_acc = lax.dynamic_update_slice_in_dim(key_acc, lax.dynamic_slice_in_dim(key_acc, first_row, window, 0) + key_term, first_row, 0)
        value_acc = lax.dynamic_update_slice_in_dim(value_acc, lax.dynamic_slice_in_dim(value_acc, first_row, window, 0) + value_term, first_row, 0)
        return (key_acc, value_acc), (out_block, query_block_grad)

    start_grads = (jnp.zeros((reach_rows + TOKENS, KVHEADS, HDIM), jnp.float32), jnp.zeros((reach_rows + TOKENS, KVHEADS, HDIM), jnp.float32))
    final_grads, block_outs = lax.scan(one_block, start_grads, jnp.arange(TOKENS // ROWS, dtype=jnp.int32))
    attention_out = block_outs[0].reshape(TOKENS, QHEADS * HDIM)
    query_grad = block_outs[1].reshape(TOKENS, QHEADS * HDIM)
    key_grad = final_grads[0][reach_rows:].astype(jnp.bfloat16).reshape(TOKENS, KVHEADS * HDIM)
    value_grad = final_grads[1][reach_rows:].astype(jnp.bfloat16).reshape(TOKENS, KVHEADS * HDIM)
    return (attention_out, query_grad, key_grad, value_grad)
```

```python
import functools
import math

import jax
import jax.numpy as jnp
from jax import lax
from jax.experimental import pallas as pl
from jax.experimental.pallas import tpu as pltpu
from jax.sharding import Mesh, PartitionSpec as P

HDIM = 128
ROWS = 384
PART = 96
HEADS = 8
QW = HEADS * HDIM
KVW = 4 * HDIM
WINDOW = 4 * ROWS
TILE = 128
KT = 256
MASKED = -1e30
SCALE = HDIM**-0.5
EXP_SCALE = SCALE * math.log2(math.e)
ANY = pl.BlockSpec(memory_space=pl.ANY)
SMEM = pl.BlockSpec(memory_space=pltpu.SMEM)
VMEM = pl.BlockSpec(memory_space=pltpu.VMEM)
BF16, F32 = jnp.bfloat16, jnp.float32


def struct(shape, dtype):
    return jax.ShapeDtypeStruct(shape, dtype)


def run_copies(copies):
    for copy in copies:
        copy.start()
    for copy in copies:
        copy.wait()


def copier(sems):
    count = [0]

    def make(src, dst):
        count[0] += 1
        return pltpu.make_async_copy(src, dst, sems.at[count[0] - 1])

    return make


def pack_kernel(width, x_ref, a_ref, b_ref, *refs):
    outs, sems = refs[:3], refs[3]
    make = copier(sems)
    copies = []
    for p in range(1, 4):
        place = pl.multiple_of(lax.rem(x_ref[0] + p, 4) * width, width)
        for n, src in enumerate((a_ref, b_ref)):
            copies.append(make(src.at[:, pl.ds(place, width)], outs[p - 1].at[:, pl.ds(n * width, width)]))
    run_copies(copies)


def pack(x, a, b):
    width = a.shape[1] // 4
    piece = struct((PART, 2 * width), BF16)
    return pl.pallas_call(
        functools.partial(pack_kernel, width),
        in_specs=[SMEM, ANY, ANY],
        out_specs=[VMEM] * 3,
        out_shape=[piece] * 3,
        scratch_shapes=[pltpu.SemaphoreType.DMA((6,))],
        name="pack",
    )(x, a, b)


def unpack_kernel(width, x_ref, *refs):
    pieces, outs, sems = refs[:4], refs[4:6], refs[6]
    make = copier(sems)
    copies = []
    for p in range(4):
        place = pl.multiple_of(lax.rem(x_ref[0] + 4 - p, 4) * width, width)
        for n, out in enumerate(outs):
            copies.append(make(pieces[p].at[:, pl.ds(n * width, width)], out.at[:, pl.ds(place, width)]))
    run_copies(copies)


def unpack(x, pieces):
    width = pieces[0].shape[1] // 2
    whole = struct((PART, 4 * width), BF16)
    return pl.pallas_call(
        functools.partial(unpack_kernel, width),
        in_specs=[SMEM] + [ANY] * 4,
        out_specs=[VMEM] * 2,
        out_shape=[whole] * 2,
        scratch_shapes=[pltpu.SemaphoreType.DMA((8,))],
        name="unpack",
    )(x, *pieces)


def arrange_kernel(x_ref, k_ref, v_ref, r1, r2, r3, doc_ref, out_ref, sems):
    make = copier(sems)
    x = x_ref[0]
    half = KVW // 2
    own = pl.multiple_of(x * half, half)
    rows = pl.ds(pl.multiple_of(x * PART, PART), PART)
    copies = [
        make(k_ref.at[:, pl.ds(own, half)], out_ref.at[rows, pl.ds(0, half)]),
        make(v_ref.at[:, pl.ds(own, half)], out_ref.at[rows, pl.ds(half, half)]),
        make(doc_ref, out_ref.at[pl.ds(ROWS, 16)]),
    ]
    for p, ref in enumerate((r1, r2, r3)):
        place = pl.multiple_of(lax.rem(x + 3 - p, 4) * PART, PART)
        copies.append(make(ref, out_ref.at[pl.ds(place, PART)]))
    run_copies(copies)


def arrange(x, keys, values, received, docs):
    return pl.pallas_call(
        arrange_kernel,
        in_specs=[SMEM] + [ANY] * 6,
        out_specs=VMEM,
        out_shape=struct((ROWS + 16, KVW), BF16),
        scratch_shapes=[pltpu.SemaphoreType.DMA((6,))],
        name="arrange",
    )(x, keys, values, *received, docs)


def dot(a, b, contract):
    return lax.dot_general(a, b, ((contract[:1], contract[1:]), ((), ())), preferred_element_type=F32)


def attention_kernel(
    x_ref, q_ref, do_ref, q1, q2, q3, kv0, kv_b, kv_c, kv_a, docs_ref,
    o0, o1, o2, o3, own_ref, far_ref, swap_ref, next_ref,
    kv, docs_kv, qd, out, acc, s_scr, p_scr, kvt, doc_col, sems,
):
    make = copier(sems)
    x, core = x_ref[0], x_ref[1]
    slot_b, slot_a = jnp.where(core == 0, 0, 2), jnp.where(core == 0, 2, 0)
    copies = []
    for ref, slot in ((kv0, 3), (kv_c, 1), (kv_b, slot_b), (kv_a, slot_a)):
        copies.append(make(ref.at[pl.ds(0, ROWS)], kv.at[pl.ds(pl.multiple_of(slot * ROWS, ROWS), ROWS)]))
        copies.append(make(ref.at[pl.ds(ROWS, 16)], docs_kv.at[slot]))
    rows = pl.ds(pl.multiple_of(x * PART, PART), PART)
    own = pl.multiple_of(x * QW, QW)
    for n, ref in enumerate((q_ref, do_ref)):
        copies.append(make(ref.at[:, pl.ds(own, QW)], qd.at[rows, pl.ds(n * QW, QW)]))
    for p, ref in enumerate((q1, q2, q3)):
        place = pl.multiple_of(lax.rem(x + 3 - p, 4) * PART, PART)
        copies.append(make(ref, qd.at[pl.ds(place, PART)]))
    for copy in copies:
        copy.start()
    acc[...] = jnp.zeros_like(acc)
    for copy in copies:
        copy.wait()

    eye = (
        lax.broadcasted_iota(jnp.int32, (HDIM, HDIM), 0) == lax.broadcasted_iota(jnp.int32, (HDIM, HDIM), 1)
    ).astype(BF16)
    key_docs = jnp.concatenate([docs_kv[s][0:1, 0:ROWS] for s in range(4)], 1).astype(F32)
    row_docs = docs_ref[...]
    first_tile = []
    for i in range(ROWS // TILE):
        first = row_docs[0:1, i * TILE : i * TILE + 1]
        earlier = jnp.sum((key_docs < first).astype(F32)).astype(jnp.int32)
        first_tile.append(earlier // KT)
    column = jnp.transpose(jnp.broadcast_to(key_docs, (TILE, WINDOW)))
    for t in range(WINDOW // KT):

        @pl.when(t >= first_tile[0])
        def _():
            keys_at = pl.ds(t * KT, KT)
            for n in range(4):
                kvt[n, :, keys_at] = dot(eye, kv[keys_at, n * HDIM : (n + 1) * HDIM], (1, 1)).astype(BF16)

    doc_col[...] = column

    for g in range(2):
        k_cols = slice(g * HDIM, (g + 1) * HDIM)
        v_cols = slice((2 + g) * HDIM, (3 + g) * HDIM)
        for i in range(ROWS // TILE):
            tile_rows = slice(i * TILE, (i + 1) * TILE)
            heads = [(4 * g + r) * HDIM for r in range(4)]
            q = jnp.concatenate([qd[tile_rows, c : c + HDIM] for c in heads], 0)
            do = jnp.concatenate([qd[tile_rows, QW + c : QW + c + HDIM] for c in heads], 0)
            docs_row = row_docs[0:1, i * TILE : (i + 1) * TILE]
            last = (3 * ROWS + (i + 1) * TILE - 1) // KT
            lo, hi = first_tile[i], last + 1
            width = 4 * TILE

            def score(t, high):
                at = pl.ds(pl.multiple_of(t * KT, KT), KT)
                s = dot(kv[at, k_cols], q, (1, 1))
                key_at = lax.broadcasted_iota(jnp.int32, (KT, TILE), 0) + t * KT
                row_at = lax.broadcasted_iota(jnp.int32, (KT, TILE), 1) + (3 * ROWS + i * TILE)
                allowed = (doc_col[at, :] == docs_row) & (key_at <= row_at)
                s = jnp.concatenate(
                    [jnp.where(allowed, s[:, r * TILE : (r + 1) * TILE], MASKED) for r in range(4)], 1
                )
                s_scr[t] = s
                return jnp.maximum(high, jnp.max(s, 0, keepdims=True))

            high = lax.fori_loop(lo, hi, score, jnp.full((1, width), MASKED, F32))
            shift = high * EXP_SCALE

            def weigh(t, carry):
                total, o_t = carry
                at = pl.ds(pl.multiple_of(t * KT, KT), KT)
                e = jnp.exp2(s_scr[t] * EXP_SCALE - shift)
                low = e.astype(BF16)
                p_scr[t] = low
                o_t = o_t + dot(kvt[2 + g, :, at], low, (1, 0))
                return total + jnp.sum(e, 0, keepdims=True), o_t

            total, o_t = lax.fori_loop(
                lo, hi, weigh, (jnp.zeros((1, width), F32), jnp.zeros((HDIM, width), F32))
            )
            inverse = 1.0 / total
            o_t = (o_t * inverse).astype(BF16).astype(F32)
            do_t = dot(eye, do, (1, 1))
            dots = jnp.sum(do_t * o_t, 0, keepdims=True)

            def back(t, dq_t):
                at = pl.ds(pl.multiple_of(t * KT, KT), KT)
                probs = p_scr[t].astype(F32) * inverse
                dp = dot(kv[at, v_cols], do, (1, 1))
                ds = (probs * (dp - dots)).astype(BF16)
                acc[at, v_cols] += dot(probs.astype(BF16), do, (1, 0))
                acc[at, k_cols] += dot(ds, q, (1, 0))
                return dq_t + dot(kvt[g, :, at], ds, (1, 0))

            dq_t = lax.fori_loop(lo, hi, back, jnp.zeros((HDIM, width), F32)) * SCALE
            for r in range(4):
                lanes = slice(r * TILE, (r + 1) * TILE)
                out[tile_rows, heads[r] : heads[r] + HDIM] = jnp.transpose(o_t[:, lanes]).astype(BF16)
                out[tile_rows, QW + heads[r] : QW + heads[r] + HDIM] = jnp.transpose(dq_t[:, lanes]).astype(BF16)

    copies = []
    for p, ref in enumerate((o0, o1, o2, o3)):
        place = pl.multiple_of(lax.rem(x + p, 4) * PART, PART)
        copies.append(make(out.at[pl.ds(place, PART)], ref))
    for copy in copies:
        copy.start()
    half = KVW // 2

    def gradient(slot):
        part = acc[pl.ds(pl.multiple_of(slot * ROWS, ROWS), ROWS), :]
        return jnp.concatenate([part[:, :half] * SCALE, part[:, half:]], 1)

    own_ref[...] = gradient(3)
    next_ref[...] = gradient(1)
    far_ref[...] = gradient(slot_b).astype(BF16)
    swap_ref[...] = gradient(slot_a).astype(BF16)
    for copy in copies:
        copy.wait()


def attention(place, queries, out_grad, received, kv0, kv_b, kv_c, kv_a, docs):
    piece = struct((PART, 2 * QW), BF16)
    tiles = WINDOW // KT
    return pl.pallas_call(
        attention_kernel,
        in_specs=[SMEM] + [ANY] * 9 + [VMEM],
        out_specs=[ANY] * 4 + [VMEM] * 4,
        out_shape=[piece] * 4
        + [struct((ROWS, KVW), F32), struct((ROWS, KVW), BF16), struct((ROWS, KVW), BF16), struct((ROWS, KVW), F32)],
        scratch_shapes=[
            pltpu.VMEM((WINDOW, KVW), BF16),
            pltpu.VMEM((4, 16, KVW), BF16),
            pltpu.VMEM((ROWS, 2 * QW), BF16),
            pltpu.VMEM((ROWS, 2 * QW), BF16),
            pltpu.VMEM((WINDOW, KVW), F32),
            pltpu.VMEM((tiles, KT, 4 * TILE), F32),
            pltpu.VMEM((tiles, KT, 4 * TILE), BF16),
            pltpu.VMEM((4, HDIM, WINDOW), BF16),
            pltpu.VMEM((WINDOW, TILE), F32),
            pltpu.SemaphoreType.DMA((20,)),
        ],
        compiler_params=pltpu.CompilerParams(vmem_limit_bytes=40 * 1024 * 1024),
        cost_estimate=pl.CostEstimate(flops=8_000_000_000, bytes_accessed=8_000_000, transcendentals=4_000_000),
        name="attention",
    )(place, queries, out_grad, *received, kv0, kv_b, kv_c, kv_a, docs)


def around(block, distance):
    return lax.ppermute(block, "head", [(i, (i + distance) % 4) for i in range(4)])


def over_chips(block, routes):
    chips = lax.axis_size("chip")
    pairs = [
        (2 * c + k, 2 * (c + step) + to)
        for c in range(chips)
        for k, step, to in routes
        if 0 <= c + step < chips
    ]
    return lax.ppermute(block, ("chip", "core"), pairs)


def local(queries, keys, values, out_grad, doc_ids):
    x = lax.axis_index("head")
    place = jnp.stack([x, lax.axis_index("core")]).astype(jnp.int32)
    doc_number = doc_ids + 1
    docs_low = jnp.pad(doc_number.astype(BF16)[None, :], ((0, 15), (0, KVW - ROWS)))
    docs = jnp.broadcast_to(doc_number.astype(F32)[None, :], (8, ROWS))
    kv_pieces = pack(place, keys, values)
    kv_received = [around(piece, p + 1) for p, piece in enumerate(kv_pieces)]
    q_pieces = pack(place, queries, out_grad)
    q_received = [around(piece, p + 1) for p, piece in enumerate(q_pieces)]
    kv0 = arrange(place, keys, values, kv_received, docs_low)
    kv_c = over_chips(kv0, [(0, 1, 0), (1, 1, 1)])
    kv_b = over_chips(kv0, [(0, 0, 1), (1, 2, 0)])
    kv_a = over_chips(kv_c, [(0, 0, 1), (1, 0, 0)])
    o0, o1, o2, o3, own, far, swap, near = attention(
        place, queries, out_grad, q_received, kv0, kv_b, kv_c, kv_a, docs
    )
    back_a = over_chips(swap, [(0, 0, 1), (1, 0, 0)])
    near = (near + back_a.astype(F32)).astype(BF16)
    back_c = over_chips(near, [(0, -1, 0), (1, -1, 1)])
    back_b = over_chips(far, [(1, 0, 0), (0, -2, 1)])
    outs = [o0] + [around(piece, p) for p, piece in ((1, o1), (2, o2), (3, o3))]
    attention_out, query_grad = unpack(place, outs)
    total = (own + back_b.astype(F32) + back_c.astype(F32)).astype(BF16)
    parts = [lax.dynamic_slice_in_dim(total, (x + p) % 4 * PART, PART, 0) for p in range(4)]
    grads = [parts[0]] + [around(parts[p], p) for p in (1, 2, 3)]
    key_grad, value_grad = unpack(place, grads)
    return attention_out, query_grad, key_grad, value_grad


def solution(mesh):
    chips = mesh.devices.size // 8
    mesh = Mesh(mesh.devices.reshape(chips, 2, 4), ("chip", "core", "head"))
    rows = P(("chip", "core", "head"), None)
    return jax.shard_map(
        local,
        mesh=mesh,
        in_specs=(rows, rows, rows, rows, P(("chip", "core"))),
        out_specs=(rows, rows, rows, rows),
        check_vma=False,
    )
```

```python
import functools
import math

import jax
import jax.numpy as jnp
from jax import lax
from jax.experimental import pallas as pl
from jax.experimental.pallas import tpu as pltpu
from jax.sharding import Mesh, PartitionSpec as P

HDIM = 128
ROWS = 384
PART = 96
KVW = 4 * HDIM
QW = 4 * HDIM
WINDOW = 4 * ROWS
TILE = 128
KT = 256
SPAN = 3 * ROWS + TILE
MASKED = -1e30
SCALE = HDIM**-0.5
EXP_SCALE = SCALE * math.log2(math.e)
ANY = pl.BlockSpec(memory_space=pl.ANY)
SMEM = pl.BlockSpec(memory_space=pltpu.SMEM)
VMEM = pl.BlockSpec(memory_space=pltpu.VMEM)
BF16, F32 = jnp.bfloat16, jnp.float32


def struct(shape, dtype):
    return jax.ShapeDtypeStruct(shape, dtype)


def run_copies(copies):
    for copy in copies:
        copy.start()
    for copy in copies:
        copy.wait()


def copier(sems):
    count = [0]

    def make(src, dst):
        count[0] += 1
        return pltpu.make_async_copy(src, dst, sems.at[count[0] - 1])

    return make


def pack_kernel(width, x_ref, a_ref, b_ref, *refs):
    outs, sems = refs[:-1], refs[-1]
    make = copier(sems)
    copies = []
    for p in range(1, 4):
        for g in range(2):
            place = pl.multiple_of(lax.rem(x_ref[0] + p, 4) * (2 * width) + g * width, width)
            for n, src in enumerate((a_ref, b_ref)):
                at = pl.ds((2 * g + n) * width, width)
                copies.append(make(src.at[:, pl.ds(place, width)], outs[p - 1].at[:, at]))
    run_copies(copies)


def pack(x, a, b):
    width = a.shape[1] // 8
    return pl.pallas_call(
        functools.partial(pack_kernel, width),
        in_specs=[SMEM, ANY, ANY],
        out_specs=[VMEM] * 3,
        out_shape=[struct((PART, 4 * width), BF16)] * 3,
        scratch_shapes=[pltpu.SemaphoreType.DMA((12,))],
        name="pack",
    )(x, a, b)


def unpack_kernel(width, x_ref, *refs):
    parts, outs, sems = refs[:4], refs[4:-1], refs[-1]
    make = copier(sems)
    copies = []
    for p in range(4):
        for g in range(2):
            place = pl.multiple_of(lax.rem(x_ref[0] + 4 - p, 4) * (2 * width) + g * width, width)
            for n, out in enumerate(outs):
                at = pl.ds((2 * g + n) * width, width)
                copies.append(make(parts[p].at[:, at], out.at[:, pl.ds(place, width)]))
    run_copies(copies)


def unpack(x, parts):
    width = parts[0].shape[1] // 4
    whole = struct((PART, 8 * width), BF16)
    return pl.pallas_call(
        functools.partial(unpack_kernel, width),
        in_specs=[SMEM] + [ANY] * 4,
        out_specs=[VMEM] * 2,
        out_shape=[whole] * 2,
        scratch_shapes=[pltpu.SemaphoreType.DMA((16,))],
        name="unpack",
    )(x, *parts)


def arrange_kernel(x_ref, k_ref, v_ref, r1, r2, r3, doc_ref, out_ref, sems):
    make = copier(sems)
    x = x_ref[0]
    rows = pl.ds(pl.multiple_of(x * PART, PART), PART)
    copies = [make(doc_ref, out_ref.at[pl.ds(ROWS, 16)])]
    for g in range(2):
        own = pl.multiple_of(x * (2 * HDIM) + g * HDIM, HDIM)
        for n, ref in enumerate((k_ref, v_ref)):
            copies.append(make(ref.at[:, pl.ds(own, HDIM)], out_ref.at[rows, pl.ds((2 * g + n) * HDIM, HDIM)]))
    for p, ref in enumerate((r1, r2, r3)):
        place = pl.multiple_of(lax.rem(x + 3 - p, 4) * PART, PART)
        copies.append(make(ref, out_ref.at[pl.ds(place, PART)]))
    run_copies(copies)


def arrange(x, keys, values, received, docs):
    return pl.pallas_call(
        arrange_kernel,
        in_specs=[SMEM] + [ANY] * 6,
        out_specs=VMEM,
        out_shape=struct((ROWS + 16, KVW), BF16),
        scratch_shapes=[pltpu.SemaphoreType.DMA((8,))],
        name="arrange",
    )(x, keys, values, *received, docs)


def dot(a, b, contract):
    return lax.dot_general(a, b, ((contract[:1], contract[1:]), ((), ())), preferred_element_type=F32)


def attention_kernel(
    x_ref, q_ref, do_ref, q1, q2, q3, kv0, kv_b, kv_c, kv_a, docs_ref,
    o0, o1, o2, o3, own_ref, far_ref, swap_ref, next_ref,
    kv, docs_kv, qd, out, acc, s_scr, p_scr, kvt, doc_col, qs, qt, sems,
):
    make = copier(sems)
    x, core = x_ref[0], x_ref[1]
    slot_b, slot_a = jnp.where(core == 0, 0, 2), jnp.where(core == 0, 2, 0)
    copies = []
    for ref, slot in ((kv0, 3), (kv_c, 1), (kv_b, slot_b), (kv_a, slot_a)):
        copies.append(make(ref.at[pl.ds(0, ROWS)], kv.at[pl.ds(pl.multiple_of(slot * ROWS, ROWS), ROWS)]))
        copies.append(make(ref.at[pl.ds(ROWS, 16)], docs_kv.at[slot]))
    kv_copies = len(copies)
    rows = pl.ds(pl.multiple_of(x * PART, PART), PART)
    for g in range(2):
        own = pl.multiple_of(x * (2 * QW) + g * QW, QW)
        for n, ref in enumerate((q_ref, do_ref)):
            copies.append(make(ref.at[:, pl.ds(own, QW)], qd.at[rows, pl.ds((2 * g + n) * QW, QW)]))
    for p, ref in enumerate((q1, q2, q3)):
        place = pl.multiple_of(lax.rem(x + 3 - p, 4) * PART, PART)
        copies.append(make(ref, qd.at[pl.ds(place, PART)]))
    for copy in copies:
        copy.start()
    acc[...] = jnp.zeros_like(acc)
    for copy in copies[:kv_copies]:
        copy.wait()

    eye = (
        lax.broadcasted_iota(jnp.int32, (HDIM, HDIM), 0) == lax.broadcasted_iota(jnp.int32, (HDIM, HDIM), 1)
    ).astype(BF16)
    key_docs = jnp.concatenate([docs_kv[s][0:1, 0:ROWS] for s in range(4)], 1)
    row_docs = docs_ref[...]
    doc_col[...] = jnp.transpose(jnp.broadcast_to(key_docs.astype(F32), (TILE, WINDOW)))
    for t in range(WINDOW // KT):
        at = slice(t * KT, (t + 1) * KT)
        for n in range(4):
            kvt[n, :, at] = dot(eye, kv[at, n * HDIM : (n + 1) * HDIM], (1, 1)).astype(BF16)
    for copy in copies[kv_copies:]:
        copy.wait()

    width = 4 * TILE
    chunks = range(SPAN // KT)
    units = range(2 * (ROWS // TILE))
    k_cols = [slice(2 * g * HDIM, (2 * g + 1) * HDIM) for g in range(2)]
    v_cols = [slice((2 * g + 1) * HDIM, (2 * g + 2) * HDIM) for g in range(2)]
    state = [{} for _ in units]

    def keys_of(u, c):
        first = u // 2 * TILE + c * KT
        return slice(first, first + KT)

    def rows_of(u):
        return slice(u // 2 * TILE, (u // 2 + 1) * TILE)

    def head_cols(u, n, r):
        first = (u % 2 * 2 + n) * QW + r * HDIM
        return slice(first, first + HDIM)

    def begin(u):
        q = jnp.concatenate([qd[rows_of(u), head_cols(u, 0, r)] for r in range(4)], 0)
        do = jnp.concatenate([qd[rows_of(u), head_cols(u, 1, r)] for r in range(4)], 0)
        qs[u, 0], qs[u, 1] = q, do
        qt[u, 0] = dot(eye, q, (1, 1)).astype(BF16)
        qt[u, 1] = dot(eye, do, (1, 1)).astype(BF16)
        state[u]["high"] = jnp.full((1, width), MASKED, F32)

    def score(u, c):
        at = keys_of(u, c)
        s = dot(kv[at, k_cols[u % 2]], qt[u, 0], (1, 0))
        docs_row = row_docs[0:1, rows_of(u)]
        allowed = doc_col[at, :] == docs_row
        if (c + 1) * KT > SPAN - TILE:
            key_at = lax.broadcasted_iota(jnp.int32, (KT, TILE), 0) + (u // 2 * TILE + c * KT)
            row_at = lax.broadcasted_iota(jnp.int32, (KT, TILE), 1) + (3 * ROWS + u // 2 * TILE)
            allowed = allowed & (key_at <= row_at)
        s = jnp.concatenate([jnp.where(allowed, s[:, r * TILE : (r + 1) * TILE], MASKED) for r in range(4)], 1)
        s_scr[u % 2, c] = s
        state[u]["high"] = jnp.maximum(state[u]["high"], jnp.max(s, 0, keepdims=True))

    def begin_weigh(u):
        state[u]["shift"] = state[u]["high"] * EXP_SCALE
        state[u]["total"] = jnp.zeros((1, width), F32)
        state[u]["o"] = jnp.zeros((HDIM, width), F32)

    def weigh(u, c):
        e = jnp.exp2(s_scr[u % 2, c] * EXP_SCALE - state[u]["shift"])
        low = e.astype(BF16)
        p_scr[u % 2, c] = low
        state[u]["total"] += jnp.sum(e, 0, keepdims=True)
        state[u]["o"] += dot(kvt[2 * (u % 2) + 1, :, keys_of(u, c)], low, (1, 0))

    def begin_back(u):
        inverse = 1.0 / state[u]["total"]
        o_t = (state[u]["o"] * inverse).astype(BF16).astype(F32)
        state[u]["inverse"] = inverse
        state[u]["dots"] = jnp.sum(qt[u, 1].astype(F32) * o_t, 0, keepdims=True)
        state[u]["dq"] = jnp.zeros((HDIM, width), F32)
        for r in range(4):
            lanes = slice(r * TILE, (r + 1) * TILE)
            out[rows_of(u), head_cols(u, 0, r)] = jnp.transpose(o_t[:, lanes]).astype(BF16)

    def back(u, c):
        at = keys_of(u, c)
        probs = p_scr[u % 2, c].astype(F32) * state[u]["inverse"]
        dp = dot(kv[at, v_cols[u % 2]], qt[u, 1], (1, 0))
        ds = (probs * (dp - state[u]["dots"])).astype(BF16)
        acc[at, v_cols[u % 2]] += dot(probs.astype(BF16), qs[u, 1], (1, 0))
        acc[at, k_cols[u % 2]] += dot(ds, qs[u, 0], (1, 0))
        state[u]["dq"] += dot(kvt[2 * (u % 2), :, at], ds, (1, 0))

    def end_back(u):
        for r in range(4):
            lanes = slice(r * TILE, (r + 1) * TILE)
            out[rows_of(u), head_cols(u, 1, r)] = jnp.transpose(state[u]["dq"][:, lanes] * SCALE).astype(BF16)

    for u in units:
        begin(u)
    for c in chunks:
        score(0, c)
    begin_weigh(0)
    for c in chunks:
        weigh(0, c)
    for u in units:
        begin_back(u)
        later = []
        if u + 1 < len(units):
            later = [functools.partial(score, u + 1, c) for c in chunks]
            later.append(functools.partial(begin_weigh, u + 1))
            later += [functools.partial(weigh, u + 1, c) for c in chunks]
        for c in chunks:
            back(u, c)
            for _ in range(3 if c == 0 else 2):
                if later:
                    later.pop(0)()
        end_back(u)

    copies = []
    for p, ref in enumerate((o0, o1, o2, o3)):
        place = pl.multiple_of(lax.rem(x + p, 4) * PART, PART)
        copies.append(make(out.at[pl.ds(place, PART)], ref))
    for copy in copies:
        copy.start()

    def gradient(slot):
        part = acc[pl.ds(pl.multiple_of(slot * ROWS, ROWS), ROWS), :]
        scales = (SCALE, 1.0, SCALE, 1.0)
        return jnp.concatenate([part[:, n * HDIM : (n + 1) * HDIM] * scales[n] for n in range(4)], 1)

    own_ref[...] = gradient(3)
    next_ref[...] = gradient(1)
    far_ref[...] = gradient(slot_b).astype(BF16)
    swap_ref[...] = gradient(slot_a).astype(BF16)
    for copy in copies:
        copy.wait()


def attention(place, queries, out_grad, received, kv0, kv_b, kv_c, kv_a, docs):
    piece = struct((PART, 4 * QW), BF16)
    grad, low_grad = struct((ROWS, KVW), F32), struct((ROWS, KVW), BF16)
    units, chunks, width = 2 * (ROWS // TILE), SPAN // KT, 4 * TILE
    return pl.pallas_call(
        attention_kernel,
        in_specs=[SMEM] + [ANY] * 9 + [VMEM],
        out_specs=[ANY] * 4 + [VMEM] * 4,
        out_shape=[piece] * 4 + [grad, low_grad, low_grad, grad],
        scratch_shapes=[
            pltpu.VMEM((WINDOW, KVW), BF16),
            pltpu.VMEM((4, 16, KVW), BF16),
            pltpu.VMEM((ROWS, 4 * QW), BF16),
            pltpu.VMEM((ROWS, 4 * QW), BF16),
            pltpu.VMEM((WINDOW, KVW), F32),
            pltpu.VMEM((2, chunks, KT, width), F32),
            pltpu.VMEM((2, chunks, KT, width), BF16),
            pltpu.VMEM((4, HDIM, WINDOW), BF16),
            pltpu.VMEM((WINDOW, TILE), F32),
            pltpu.VMEM((units, 2, width, HDIM), BF16),
            pltpu.VMEM((units, 2, HDIM, width), BF16),
            pltpu.SemaphoreType.DMA((20,)),
        ],
        compiler_params=pltpu.CompilerParams(vmem_limit_bytes=40 * 1024 * 1024),
        cost_estimate=pl.CostEstimate(flops=8_000_000_000, bytes_accessed=8_000_000, transcendentals=4_000_000),
        name="attention",
    )(place, queries, out_grad, *received, kv0, kv_b, kv_c, kv_a, docs)


def around(block, distance):
    return lax.ppermute(block, "head", [(i, (i + distance) % 4) for i in range(4)])


def over_chips(block, routes):
    chips = lax.axis_size("chip")
    pairs = [
        (2 * c + k, 2 * (c + step) + to)
        for c in range(chips)
        for k, step, to in routes
        if 0 <= c + step < chips
    ]
    return lax.ppermute(block, ("chip", "core"), pairs)


def local(queries, keys, values, out_grad, doc_ids):
    x = lax.axis_index("head")
    place = jnp.stack([x, lax.axis_index("core")]).astype(jnp.int32)
    doc_number = doc_ids + 1
    docs_low = jnp.pad(doc_number.astype(BF16)[None, :], ((0, 15), (0, KVW - ROWS)))
    docs = jnp.broadcast_to(doc_number.astype(F32)[None, :], (8, ROWS))
    kv_received = [around(piece, p + 1) for p, piece in enumerate(pack(place, keys, values))]
    q_pieces = pack(place, queries, out_grad)
    kv_received, q_pieces = lax.optimization_barrier((kv_received, q_pieces))
    q_received = [around(piece, p + 1) for p, piece in enumerate(q_pieces)]
    kv0 = arrange(place, keys, values, kv_received, docs_low)
    kv_c = over_chips(kv0, [(0, 1, 0), (1, 1, 1)])
    kv_b = over_chips(kv0, [(0, 0, 1), (1, 2, 0)])
    kv_c, q_received = lax.optimization_barrier((kv_c, q_received))
    kv_a = over_chips(kv_c, [(0, 0, 1), (1, 0, 0)])
    o0, o1, o2, o3, own, far, swap, near = attention(
        place, queries, out_grad, q_received, kv0, kv_b, kv_c, kv_a, docs
    )
    back_a = over_chips(swap, [(0, 0, 1), (1, 0, 0)])
    near = (near + back_a.astype(F32)).astype(BF16)
    back_c = over_chips(near, [(0, -1, 0), (1, -1, 1)])
    back_b = over_chips(far, [(1, 0, 0), (0, -2, 1)])
    outs = [o0] + [around(piece, p) for p, piece in ((1, o1), (2, o2), (3, o3))]
    attention_out, query_grad = unpack(place, outs)
    total = (own + back_b.astype(F32) + back_c.astype(F32)).astype(BF16)
    parts = [lax.dynamic_slice_in_dim(total, (x + p) % 4 * PART, PART, 0) for p in range(4)]
    grads = [parts[0]] + [around(parts[p], p) for p in (1, 2, 3)]
    key_grad, value_grad = unpack(place, grads)
    return attention_out, query_grad, key_grad, value_grad


def solution(mesh):
    chips = mesh.devices.size // 8
    mesh = Mesh(mesh.devices.reshape(chips, 2, 4), ("chip", "core", "head"))
    rows = P(("chip", "core", "head"), None)
    return jax.shard_map(
        local,
        mesh=mesh,
        in_specs=(rows, rows, rows, rows, P(("chip", "core"))),
        out_specs=(rows, rows, rows, rows),
        check_vma=False,
    )
```

```python
import functools
import math

import jax
import jax.numpy as jnp
from jax import lax
from jax.experimental import pallas as pl
from jax.experimental.pallas import tpu as pltpu
from jax.sharding import Mesh, PartitionSpec as P

HDIM = 128
ROWS = 384
PART = 96
KVW = 4 * HDIM
QW = 4 * HDIM
WINDOW = 4 * ROWS
TILE = 128
KT = 256
SPAN = 3 * ROWS + TILE
MASKED = -1e30
SCALE = HDIM**-0.5
EXP_SCALE = SCALE * math.log2(math.e)
SMALL = pltpu.CompilerParams(vmem_limit_bytes=4 * 1024 * 1024)
ANY = pl.BlockSpec(memory_space=pl.ANY)
SMEM = pl.BlockSpec(memory_space=pltpu.SMEM)
HBM = pl.BlockSpec(memory_space=pltpu.HBM)
VMEM = pl.BlockSpec(memory_space=pltpu.VMEM)
BF16, F32 = jnp.bfloat16, jnp.float32


def struct(shape, dtype):
    return jax.ShapeDtypeStruct(shape, dtype)


def run_copies(copies):
    for copy in copies:
        copy.start()
    for copy in copies:
        copy.wait()


def copier(sems):
    count = [0]

    def make(src, dst):
        count[0] += 1
        return pltpu.make_async_copy(src, dst, sems.at[count[0] - 1])

    return make


def pack_kernel(width, x_ref, a_ref, b_ref, *refs):
    outs, sems = refs[:-1], refs[-1]
    make = copier(sems)
    copies = []
    for p in range(1, 4):
        for g in range(2):
            place = pl.multiple_of(lax.rem(x_ref[0] + p, 4) * (2 * width) + g * width, width)
            for n, src in enumerate((a_ref, b_ref)):
                at = pl.ds((2 * g + n) * width, width)
                copies.append(make(src.at[:, pl.ds(place, width)], outs[p - 1].at[:, at]))
    run_copies(copies)


def pack(x, a, b):
    width = a.shape[1] // 8
    return pl.pallas_call(
        functools.partial(pack_kernel, width),
        in_specs=[SMEM, ANY, ANY],
        out_specs=[VMEM] * 3,
        out_shape=[struct((PART, 4 * width), BF16)] * 3,
        scratch_shapes=[pltpu.SemaphoreType.DMA((12,))],
        compiler_params=SMALL,
        name="pack",
    )(x, a, b)


def cut(x, a, b):
    width = a.shape[1] // 8
    pieces = []
    for p in range(1, 4):
        place = (x + p) % 4 * (2 * width)
        cuts = [lax.dynamic_slice_in_dim(src, place + g * width, width, 1) for g in range(2) for src in (a, b)]
        pieces.append(jnp.concatenate(cuts, 1))
    return pieces


def unpack_kernel(width, x_ref, *refs):
    parts, outs, sems = refs[:4], refs[4:-1], refs[-1]
    make = copier(sems)
    copies = []
    for p in range(4):
        for g in range(2):
            place = pl.multiple_of(lax.rem(x_ref[0] + 4 - p, 4) * (2 * width) + g * width, width)
            for n, out in enumerate(outs):
                at = pl.ds((2 * g + n) * width, width)
                copies.append(make(parts[p].at[:, at], out.at[:, pl.ds(place, width)]))
    run_copies(copies)


def unpack(x, parts):
    width = parts[0].shape[1] // 4
    whole = struct((PART, 8 * width), BF16)
    return pl.pallas_call(
        functools.partial(unpack_kernel, width),
        in_specs=[SMEM] + [ANY] * 4,
        out_specs=[VMEM] * 2,
        out_shape=[whole] * 2,
        scratch_shapes=[pltpu.SemaphoreType.DMA((16,))],
        compiler_params=SMALL,
        name="unpack",
    )(x, *parts)


def arrange_kernel(x_ref, k_ref, v_ref, r1, r2, r3, doc_ref, out_ref, sems):
    make = copier(sems)
    x = x_ref[0]
    rows = pl.ds(pl.multiple_of(x * PART, PART), PART)
    copies = [make(doc_ref, out_ref.at[pl.ds(ROWS, 16)])]
    for g in range(2):
        own = pl.multiple_of(x * (2 * HDIM) + g * HDIM, HDIM)
        for n, ref in enumerate((k_ref, v_ref)):
            copies.append(make(ref.at[:, pl.ds(own, HDIM)], out_ref.at[rows, pl.ds((2 * g + n) * HDIM, HDIM)]))
    for p, ref in enumerate((r1, r2, r3)):
        place = pl.multiple_of(lax.rem(x + 3 - p, 4) * PART, PART)
        copies.append(make(ref, out_ref.at[pl.ds(place, PART)]))
    run_copies(copies)


def arrange(x, keys, values, received, docs):
    return pl.pallas_call(
        arrange_kernel,
        in_specs=[SMEM] + [ANY] * 6,
        out_specs=VMEM,
        out_shape=struct((ROWS + 16, KVW), BF16),
        scratch_shapes=[pltpu.SemaphoreType.DMA((8,))],
        compiler_params=SMALL,
        name="arrange",
    )(x, keys, values, *received, docs)


def dot(a, b, contract):
    return lax.dot_general(a, b, ((contract[:1], contract[1:]), ((), ())), preferred_element_type=F32)


def attention_kernel(
    x_ref, q_ref, do_ref, q1, q2, q3, kv0, kv_b, kv_c, kv_a, docs_ref,
    o0, o1, o2, o3, own_ref, far_ref, swap_ref, next_ref,
    kv, docs_kv, qd, out, acc, s_scr, p_scr, kvt, doc_col, qs, qt, sems,
):
    make = copier(sems)
    x, core = x_ref[0], x_ref[1]
    slot_b, slot_a = jnp.where(core == 0, 0, 2), jnp.where(core == 0, 2, 0)
    copies = []
    for ref, slot in ((kv0, 3), (kv_c, 1), (kv_b, slot_b), (kv_a, slot_a)):
        copies.append(make(ref.at[pl.ds(0, ROWS)], kv.at[pl.ds(pl.multiple_of(slot * ROWS, ROWS), ROWS)]))
        copies.append(make(ref.at[pl.ds(ROWS, 16)], docs_kv.at[slot]))
    kv_copies = len(copies)
    rows = pl.ds(pl.multiple_of(x * PART, PART), PART)
    for g in range(2):
        own = pl.multiple_of(x * (2 * QW) + g * QW, QW)
        for n, ref in enumerate((q_ref, do_ref)):
            copies.append(make(ref.at[:, pl.ds(own, QW)], qd.at[rows, pl.ds((2 * g + n) * QW, QW)]))
    for p, ref in enumerate((q1, q2, q3)):
        place = pl.multiple_of(lax.rem(x + 3 - p, 4) * PART, PART)
        copies.append(make(ref, qd.at[pl.ds(place, PART)]))
    for copy in copies:
        copy.start()
    acc[...] = jnp.zeros_like(acc)
    for copy in copies[:kv_copies]:
        copy.wait()

    eye = (
        lax.broadcasted_iota(jnp.int32, (HDIM, HDIM), 0) == lax.broadcasted_iota(jnp.int32, (HDIM, HDIM), 1)
    ).astype(BF16)
    key_docs = jnp.concatenate([docs_kv[s][0:1, 0:ROWS] for s in range(4)], 1)
    row_docs = docs_ref[...]
    doc_col[...] = jnp.transpose(jnp.broadcast_to(key_docs.astype(F32), (TILE, WINDOW)))
    for t in range(WINDOW // KT):
        at = slice(t * KT, (t + 1) * KT)
        for n in range(4):
            kvt[n, :, at] = dot(eye, kv[at, n * HDIM : (n + 1) * HDIM], (1, 1)).astype(BF16)
    for copy in copies[kv_copies:]:
        copy.wait()

    width = 4 * TILE
    chunks = range(SPAN // KT)
    units = range(2 * (ROWS // TILE))
    k_cols = [slice(2 * g * HDIM, (2 * g + 1) * HDIM) for g in range(2)]
    v_cols = [slice((2 * g + 1) * HDIM, (2 * g + 2) * HDIM) for g in range(2)]
    state = [{} for _ in units]

    def keys_of(u, c):
        first = u // 2 * TILE + c * KT
        return slice(first, first + KT)

    def rows_of(u):
        return slice(u // 2 * TILE, (u // 2 + 1) * TILE)

    def head_cols(u, n, r):
        first = (u % 2 * 2 + n) * QW + r * HDIM
        return slice(first, first + HDIM)

    def begin(u):
        q = jnp.concatenate([qd[rows_of(u), head_cols(u, 0, r)] for r in range(4)], 0)
        do = jnp.concatenate([qd[rows_of(u), head_cols(u, 1, r)] for r in range(4)], 0)
        qs[u, 0], qs[u, 1] = q, do
        qt[u, 0] = dot(eye, q, (1, 1)).astype(BF16)
        qt[u, 1] = dot(eye, do, (1, 1)).astype(BF16)
        state[u]["high"] = jnp.full((1, width), MASKED, F32)

    def score(u, c):
        at = keys_of(u, c)
        s = dot(kv[at, k_cols[u % 2]], qt[u, 0], (1, 0))
        docs_row = row_docs[0:1, rows_of(u)]
        allowed = doc_col[at, :] == docs_row
        if (c + 1) * KT > SPAN - TILE:
            key_at = lax.broadcasted_iota(jnp.int32, (KT, TILE), 0) + (u // 2 * TILE + c * KT)
            row_at = lax.broadcasted_iota(jnp.int32, (KT, TILE), 1) + (3 * ROWS + u // 2 * TILE)
            allowed = allowed & (key_at <= row_at)
        s = jnp.concatenate([jnp.where(allowed, s[:, r * TILE : (r + 1) * TILE], MASKED) for r in range(4)], 1)
        s_scr[u % 2, c] = s
        state[u]["high"] = jnp.maximum(state[u]["high"], jnp.max(s, 0, keepdims=True))

    def begin_weigh(u):
        state[u]["shift"] = state[u]["high"] * EXP_SCALE
        state[u]["total"] = jnp.zeros((1, width), F32)
        state[u]["o"] = jnp.zeros((HDIM, width), F32)

    def weigh(u, c):
        e = jnp.exp2(s_scr[u % 2, c] * EXP_SCALE - state[u]["shift"])
        low = e.astype(BF16)
        p_scr[u % 2, c] = low
        state[u]["total"] += jnp.sum(e, 0, keepdims=True)
        state[u]["o"] += dot(kvt[2 * (u % 2) + 1, :, keys_of(u, c)], low, (1, 0))

    def begin_back(u):
        inverse = 1.0 / state[u]["total"]
        o_t = (state[u]["o"] * inverse).astype(BF16).astype(F32)
        state[u]["inverse"] = inverse
        state[u]["dots"] = jnp.sum(qt[u, 1].astype(F32) * o_t, 0, keepdims=True)
        state[u]["dq"] = jnp.zeros((HDIM, width), F32)
        for r in range(4):
            lanes = slice(r * TILE, (r + 1) * TILE)
            out[rows_of(u), head_cols(u, 0, r)] = jnp.transpose(o_t[:, lanes]).astype(BF16)

    def back(u, c):
        at = keys_of(u, c)
        probs = p_scr[u % 2, c].astype(F32) * state[u]["inverse"]
        dp = dot(kv[at, v_cols[u % 2]], qt[u, 1], (1, 0))
        ds = (probs * (dp - state[u]["dots"])).astype(BF16)
        acc[at, v_cols[u % 2]] += dot(probs.astype(BF16), qs[u, 1], (1, 0))
        acc[at, k_cols[u % 2]] += dot(ds, qs[u, 0], (1, 0))
        state[u]["dq"] += dot(kvt[2 * (u % 2), :, at], ds, (1, 0))

    def end_back(u):
        for r in range(4):
            lanes = slice(r * TILE, (r + 1) * TILE)
            out[rows_of(u), head_cols(u, 1, r)] = jnp.transpose(state[u]["dq"][:, lanes] * SCALE).astype(BF16)

    for u in units:
        begin(u)
    for c in chunks:
        score(0, c)
    begin_weigh(0)
    for c in chunks:
        weigh(0, c)
    for u in units:
        begin_back(u)
        later = []
        if u + 1 < len(units):
            later = [functools.partial(score, u + 1, c) for c in chunks]
            later.append(functools.partial(begin_weigh, u + 1))
            later += [functools.partial(weigh, u + 1, c) for c in chunks]
        for c in chunks:
            back(u, c)
            for _ in range(3 if c == 0 else 2):
                if later:
                    later.pop(0)()
        end_back(u)

    copies = []
    for p, ref in enumerate((o0, o1, o2, o3)):
        place = pl.multiple_of(lax.rem(x + p, 4) * PART, PART)
        copies.append(make(out.at[pl.ds(place, PART)], ref))
    for copy in copies:
        copy.start()

    def gradient(slot):
        part = acc[pl.ds(pl.multiple_of(slot * ROWS, ROWS), ROWS), :]
        scales = (SCALE, 1.0, SCALE, 1.0)
        return jnp.concatenate([part[:, n * HDIM : (n + 1) * HDIM] * scales[n] for n in range(4)], 1)

    own_ref[...] = gradient(3)
    next_ref[...] = gradient(1)
    far_ref[...] = gradient(slot_b).astype(BF16)
    swap_ref[...] = gradient(slot_a).astype(BF16)
    for copy in copies:
        copy.wait()


def attention(place, queries, out_grad, received, kv0, kv_b, kv_c, kv_a, docs):
    piece = struct((PART, 4 * QW), BF16)
    grad, low_grad = struct((ROWS, KVW), F32), struct((ROWS, KVW), BF16)
    units, chunks, width = 2 * (ROWS // TILE), SPAN // KT, 4 * TILE
    return pl.pallas_call(
        attention_kernel,
        in_specs=[SMEM] + [ANY] * 9 + [VMEM],
        out_specs=[ANY] * 4 + [VMEM] * 4,
        out_shape=[piece] * 4 + [grad, low_grad, low_grad, grad],
        scratch_shapes=[
            pltpu.VMEM((WINDOW, KVW), BF16),
            pltpu.VMEM((4, 16, KVW), BF16),
            pltpu.VMEM((ROWS, 4 * QW), BF16),
            pltpu.VMEM((ROWS, 4 * QW), BF16),
            pltpu.VMEM((WINDOW, KVW), F32),
            pltpu.VMEM((2, chunks, KT, width), F32),
            pltpu.VMEM((2, chunks, KT, width), BF16),
            pltpu.VMEM((4, HDIM, WINDOW), BF16),
            pltpu.VMEM((WINDOW, TILE), F32),
            pltpu.VMEM((units, 2, width, HDIM), BF16),
            pltpu.VMEM((units, 2, HDIM, width), BF16),
            pltpu.SemaphoreType.DMA((20,)),
        ],
        compiler_params=pltpu.CompilerParams(vmem_limit_bytes=28 * 1024 * 1024),
        cost_estimate=pl.CostEstimate(flops=8_000_000_000, bytes_accessed=8_000_000, transcendentals=4_000_000),
        name="attention",
    )(place, queries, out_grad, *received, kv0, kv_b, kv_c, kv_a, docs)


def arrived_kernel(docs_ref, *refs):
    refs[-1][...] = docs_ref[...]


def arrived(docs, received, work):
    return pl.pallas_call(
        arrived_kernel,
        in_specs=[VMEM] + [ANY] * len(received),
        out_specs=VMEM,
        out_shape=struct(docs.shape, docs.dtype),
        compiler_params=SMALL,
        cost_estimate=pl.CostEstimate(flops=work, bytes_accessed=1_000_000, transcendentals=0),
        name="arrived",
    )(docs, *received)


def total_kernel(x_ref, own_ref, b_ref, c_ref, docs_ref, *outs):
    del docs_ref
    for p, out in enumerate(outs):
        rows = pl.ds(pl.multiple_of(lax.rem(x_ref[0] + p, 4) * PART, PART), PART)
        out[...] = (own_ref[rows] + b_ref[rows].astype(F32) + c_ref[rows].astype(F32)).astype(BF16)


def total(place, own, back_b, back_c, docs):
    return pl.pallas_call(
        total_kernel,
        in_specs=[SMEM] + [VMEM] * 4,
        out_specs=[VMEM] * 4,
        out_shape=[struct((PART, KVW), BF16)] * 4,
        compiler_params=SMALL,
        name="total",
    )(place, own, back_b, back_c, docs)


def around(block, distance):
    return lax.ppermute(block, "head", [(i, (i + distance) % 4) for i in range(4)])


def over_chips(block, routes):
    chips = lax.axis_size("chip")
    pairs = [
        (2 * c + k, 2 * (c + step) + to)
        for c in range(chips)
        for k, step, to in routes
        if 0 <= c + step < chips
    ]
    return lax.ppermute(block, ("chip", "core"), pairs)


def local(queries, keys, values, out_grad, doc_ids):
    x = lax.axis_index("head")
    place = jnp.stack([x, lax.axis_index("core")]).astype(jnp.int32)
    doc_number = doc_ids + 1
    docs_low = jnp.pad(doc_number.astype(BF16)[None, :], ((0, 15), (0, KVW - ROWS)))
    docs = jnp.broadcast_to(doc_number.astype(F32)[None, :], (8, ROWS))
    kv_received = [around(piece, p + 1) for p, piece in enumerate(cut(x, keys, values))]
    q_pieces = pack(place, queries, out_grad)
    kv_received, q_pieces = lax.optimization_barrier((kv_received, q_pieces))
    q_received = [around(piece, p + 1) for p, piece in enumerate(q_pieces)]
    kv0 = arrange(place, keys, values, kv_received, docs_low)
    kv_c = over_chips(kv0, [(0, 1, 0), (1, 1, 1)])
    kv_b = over_chips(kv0, [(0, 0, 1), (1, 2, 0)])
    kv_c, docs = lax.optimization_barrier((kv_c, arrived(docs, q_received, 40_000_000_000)))
    kv_a = over_chips(kv_c, [(0, 0, 1), (1, 0, 0)])
    o0, o1, o2, o3, own, far, swap, near = attention(
        place, queries, out_grad, q_received, kv0, kv_b, kv_c, kv_a, docs
    )
    back_a = over_chips(swap, [(0, 0, 1), (1, 0, 0)])
    near = (near + back_a.astype(F32)).astype(BF16)
    near, far = lax.optimization_barrier((near, far))
    back_b = over_chips(far, [(1, 0, 0), (0, -2, 1)])
    back_c = over_chips(near, [(0, -1, 0), (1, -1, 1)])
    outs = [o0] + [around(piece, p) for p, piece in ((1, o1), (2, o2), (3, o3))]
    docs = arrived(docs, outs[1:], 4_000_000_000)
    parts = total(place, own, back_b, back_c, docs)
    grads = [parts[0]] + [around(parts[p], p) for p in (1, 2, 3)]
    attention_out, query_grad = unpack(place, outs)
    key_grad, value_grad = unpack(place, grads)
    return attention_out, query_grad, key_grad, value_grad


def solution(mesh):
    chips = mesh.devices.size // 8
    mesh = Mesh(mesh.devices.reshape(chips, 2, 4), ("chip", "core", "head"))
    rows = P(("chip", "core", "head"), None)
    return jax.shard_map(
        local,
        mesh=mesh,
        in_specs=(rows, rows, rows, rows, P(("chip", "core"))),
        out_specs=(rows, rows, rows, rows),
        check_vma=False,
    )
```

```python
import functools
import math

import jax
import jax.numpy as jnp
from jax import lax
from jax.experimental import pallas as pl
from jax.experimental.pallas import tpu as pltpu
from jax.sharding import Mesh, PartitionSpec as P

HDIM = 128
ROWS = 384
PART = 96
KVW = 4 * HDIM
QW = 4 * HDIM
WINDOW = 4 * ROWS
TILE = 128
KT = 256
SPAN = 3 * ROWS + TILE
MASKED = -1e30
SCALE = HDIM**-0.5
EXP_SCALE = SCALE * math.log2(math.e)
SMALL = pltpu.CompilerParams(vmem_limit_bytes=4 * 1024 * 1024)
ANY = pl.BlockSpec(memory_space=pl.ANY)
SMEM = pl.BlockSpec(memory_space=pltpu.SMEM)
HBM = pl.BlockSpec(memory_space=pltpu.HBM)
VMEM = pl.BlockSpec(memory_space=pltpu.VMEM)
BF16, F32 = jnp.bfloat16, jnp.float32


def struct(shape, dtype):
    return jax.ShapeDtypeStruct(shape, dtype)


def run_copies(copies):
    for copy in copies:
        copy.start()
    for copy in copies:
        copy.wait()


def copier(sems):
    count = [0]

    def make(src, dst):
        count[0] += 1
        return pltpu.make_async_copy(src, dst, sems.at[count[0] - 1])

    return make


def pack_kernel(width, x_ref, a_ref, b_ref, *refs):
    outs, sems = refs[:-1], refs[-1]
    make = copier(sems)
    copies = []
    for p in range(1, 4):
        for g in range(2):
            place = pl.multiple_of(lax.rem(x_ref[0] + p, 4) * (2 * width) + g * width, width)
            for n, src in enumerate((a_ref, b_ref)):
                at = pl.ds((2 * g + n) * width, width)
                copies.append(make(src.at[:, pl.ds(place, width)], outs[p - 1].at[:, at]))
    run_copies(copies)


def pack(x, a, b):
    width = a.shape[1] // 8
    return pl.pallas_call(
        functools.partial(pack_kernel, width),
        in_specs=[SMEM, ANY, ANY],
        out_specs=[VMEM] * 3,
        out_shape=[struct((PART, 4 * width), BF16)] * 3,
        scratch_shapes=[pltpu.SemaphoreType.DMA((12,))],
        compiler_params=SMALL,
        name="pack",
    )(x, a, b)


def cut(x, a, b):
    width = a.shape[1] // 8
    pieces = []
    for p in range(4):
        place = (x + p) % 4 * (2 * width)
        cuts = [lax.dynamic_slice_in_dim(src, place + g * width, width, 1) for g in range(2) for src in (a, b)]
        pieces.append(jnp.concatenate(cuts, 1))
    return pieces


def unpack_kernel(width, x_ref, *refs):
    parts, outs, sems = refs[:4], refs[4:-1], refs[-1]
    make = copier(sems)
    copies = []
    for p in range(4):
        for g in range(2):
            place = pl.multiple_of(lax.rem(x_ref[0] + 4 - p, 4) * (2 * width) + g * width, width)
            for n, out in enumerate(outs):
                at = pl.ds((2 * g + n) * width, width)
                copies.append(make(parts[p].at[:, at], out.at[:, pl.ds(place, width)]))
    run_copies(copies)


def unpack(x, parts):
    width = parts[0].shape[1] // 4
    whole = struct((PART, 8 * width), BF16)
    return pl.pallas_call(
        functools.partial(unpack_kernel, width),
        in_specs=[SMEM] + [ANY] * 4,
        out_specs=[VMEM] * 2,
        out_shape=[whole] * 2,
        scratch_shapes=[pltpu.SemaphoreType.DMA((16,))],
        compiler_params=SMALL,
        name="unpack",
    )(x, *parts)


def dot(a, b, contract):
    return lax.dot_general(a, b, ((contract[:1], contract[1:]), ((), ())), preferred_element_type=F32)


def attention_kernel(
    x_ref, q_ref, do_ref, q1, q2, q3, kv0, kv_b, kv_c, kv_a, docs_ref,
    o0, o1, o2, o3, own_ref, far_ref, swap_ref, next_ref,
    kv, docs_kv, qd, out, acc, s_scr, p_scr, kvt, doc_col, qs, qt, sems,
):
    make = copier(sems)
    x, core = x_ref[0], x_ref[1]
    slot_b, slot_a = jnp.where(core == 0, 0, 2), jnp.where(core == 0, 2, 0)
    copies = []
    for ref, slot in ((kv0, 3), (kv_c, 1), (kv_b, slot_b), (kv_a, slot_a)):
        copies.append(make(ref.at[pl.ds(0, ROWS)], kv.at[pl.ds(pl.multiple_of(slot * ROWS, ROWS), ROWS)]))
        copies.append(make(ref.at[pl.ds(ROWS, 16)], docs_kv.at[slot]))
    kv_copies = len(copies)
    rows = pl.ds(pl.multiple_of(x * PART, PART), PART)
    for g in range(2):
        own = pl.multiple_of(x * (2 * QW) + g * QW, QW)
        for n, ref in enumerate((q_ref, do_ref)):
            copies.append(make(ref.at[:, pl.ds(own, QW)], qd.at[rows, pl.ds((2 * g + n) * QW, QW)]))
    for p, ref in enumerate((q1, q2, q3)):
        place = pl.multiple_of(lax.rem(x + 3 - p, 4) * PART, PART)
        copies.append(make(ref, qd.at[pl.ds(place, PART)]))
    for copy in copies:
        copy.start()
    acc[...] = jnp.zeros_like(acc)
    for copy in copies[:kv_copies]:
        copy.wait()

    eye = (
        lax.broadcasted_iota(jnp.int32, (HDIM, HDIM), 0) == lax.broadcasted_iota(jnp.int32, (HDIM, HDIM), 1)
    ).astype(BF16)
    key_docs = jnp.concatenate([docs_kv[s][0:1, 0:ROWS] for s in range(4)], 1)
    row_docs = docs_ref[...]
    doc_col[...] = jnp.transpose(jnp.broadcast_to(key_docs.astype(F32), (TILE, WINDOW)))
    for t in range(WINDOW // KT):
        at = slice(t * KT, (t + 1) * KT)
        for n in range(4):
            kvt[n, :, at] = dot(eye, kv[at, n * HDIM : (n + 1) * HDIM], (1, 1)).astype(BF16)
    for copy in copies[kv_copies:]:
        copy.wait()

    width = 4 * TILE
    chunks = range(SPAN // KT)
    units = range(2 * (ROWS // TILE))
    k_cols = [slice(2 * g * HDIM, (2 * g + 1) * HDIM) for g in range(2)]
    v_cols = [slice((2 * g + 1) * HDIM, (2 * g + 2) * HDIM) for g in range(2)]
    state = [{} for _ in units]

    def keys_of(u, c):
        first = u // 2 * TILE + c * KT
        return slice(first, first + KT)

    def rows_of(u):
        return slice(u // 2 * TILE, (u // 2 + 1) * TILE)

    def head_cols(u, n, r):
        first = (u % 2 * 2 + n) * QW + r * HDIM
        return slice(first, first + HDIM)

    def begin(u):
        q = jnp.concatenate([qd[rows_of(u), head_cols(u, 0, r)] for r in range(4)], 0)
        do = jnp.concatenate([qd[rows_of(u), head_cols(u, 1, r)] for r in range(4)], 0)
        qs[u, 0], qs[u, 1] = q, do
        qt[u, 0] = dot(eye, q, (1, 1)).astype(BF16)
        qt[u, 1] = dot(eye, do, (1, 1)).astype(BF16)
        state[u]["high"] = jnp.full((1, width), MASKED, F32)

    def score(u, c):
        at = keys_of(u, c)
        s = dot(kv[at, k_cols[u % 2]], qt[u, 0], (1, 0))
        docs_row = row_docs[0:1, rows_of(u)]
        allowed = doc_col[at, :] == docs_row
        if (c + 1) * KT > SPAN - TILE:
            key_at = lax.broadcasted_iota(jnp.int32, (KT, TILE), 0) + (u // 2 * TILE + c * KT)
            row_at = lax.broadcasted_iota(jnp.int32, (KT, TILE), 1) + (3 * ROWS + u // 2 * TILE)
            allowed = allowed & (key_at <= row_at)
        s = jnp.concatenate([jnp.where(allowed, s[:, r * TILE : (r + 1) * TILE], MASKED) for r in range(4)], 1)
        s_scr[u % 2, c] = s
        state[u]["high"] = jnp.maximum(state[u]["high"], jnp.max(s, 0, keepdims=True))

    def begin_weigh(u):
        state[u]["shift"] = state[u]["high"] * EXP_SCALE
        state[u]["total"] = jnp.zeros((1, width), F32)
        state[u]["o"] = jnp.zeros((HDIM, width), F32)

    def weigh(u, c):
        e = jnp.exp2(s_scr[u % 2, c] * EXP_SCALE - state[u]["shift"])
        low = e.astype(BF16)
        p_scr[u % 2, c] = low
        state[u]["total"] += jnp.sum(e, 0, keepdims=True)
        state[u]["o"] += dot(kvt[2 * (u % 2) + 1, :, keys_of(u, c)], low, (1, 0))

    def begin_back(u):
        inverse = 1.0 / state[u]["total"]
        o_t = (state[u]["o"] * inverse).astype(BF16).astype(F32)
        state[u]["inverse"] = inverse
        state[u]["dots"] = jnp.sum(qt[u, 1].astype(F32) * o_t, 0, keepdims=True)
        state[u]["dq"] = jnp.zeros((HDIM, width), F32)
        for r in range(4):
            lanes = slice(r * TILE, (r + 1) * TILE)
            out[rows_of(u), head_cols(u, 0, r)] = jnp.transpose(o_t[:, lanes]).astype(BF16)

    def back(u, c):
        at = keys_of(u, c)
        probs = p_scr[u % 2, c].astype(F32) * state[u]["inverse"]
        dp = dot(kv[at, v_cols[u % 2]], qt[u, 1], (1, 0))
        ds = (probs * (dp - state[u]["dots"])).astype(BF16)
        acc[at, v_cols[u % 2]] += dot(probs.astype(BF16), qs[u, 1], (1, 0))
        acc[at, k_cols[u % 2]] += dot(ds, qs[u, 0], (1, 0))
        state[u]["dq"] += dot(kvt[2 * (u % 2), :, at], ds, (1, 0))

    def end_back(u):
        for r in range(4):
            lanes = slice(r * TILE, (r + 1) * TILE)
            out[rows_of(u), head_cols(u, 1, r)] = jnp.transpose(state[u]["dq"][:, lanes] * SCALE).astype(BF16)

    for u in units:
        begin(u)
    for c in chunks:
        score(0, c)
    begin_weigh(0)
    for c in chunks:
        weigh(0, c)
    for u in units:
        begin_back(u)
        later = []
        if u + 1 < len(units):
            later = [functools.partial(score, u + 1, c) for c in chunks]
            later.append(functools.partial(begin_weigh, u + 1))
            later += [functools.partial(weigh, u + 1, c) for c in chunks]
        for c in chunks:
            back(u, c)
            for _ in range(3 if c == 0 else 2):
                if later:
                    later.pop(0)()
        end_back(u)

    copies = []
    for p, ref in enumerate((o0, o1, o2, o3)):
        place = pl.multiple_of(lax.rem(x + p, 4) * PART, PART)
        copies.append(make(out.at[pl.ds(place, PART)], ref))
    for copy in copies:
        copy.start()

    def gradient(slot):
        part = acc[pl.ds(pl.multiple_of(slot * ROWS, ROWS), ROWS), :]
        scales = (SCALE, 1.0, SCALE, 1.0)
        return jnp.concatenate([part[:, n * HDIM : (n + 1) * HDIM] * scales[n] for n in range(4)], 1)

    own_ref[...] = gradient(3)
    next_ref[...] = gradient(1)
    far_ref[...] = gradient(slot_b).astype(BF16)
    swap_ref[...] = gradient(slot_a).astype(BF16)
    for copy in copies:
        copy.wait()


def attention(place, queries, out_grad, received, kv0, kv_b, kv_c, kv_a, docs):
    piece = struct((PART, 4 * QW), BF16)
    grad, low_grad = struct((ROWS, KVW), F32), struct((ROWS, KVW), BF16)
    units, chunks, width = 2 * (ROWS // TILE), SPAN // KT, 4 * TILE
    return pl.pallas_call(
        attention_kernel,
        in_specs=[SMEM] + [ANY] * 9 + [VMEM],
        out_specs=[ANY] * 4 + [VMEM] * 4,
        out_shape=[piece] * 4 + [grad, low_grad, low_grad, grad],
        scratch_shapes=[
            pltpu.VMEM((WINDOW, KVW), BF16),
            pltpu.VMEM((4, 16, KVW), BF16),
            pltpu.VMEM((ROWS, 4 * QW), BF16),
            pltpu.VMEM((ROWS, 4 * QW), BF16),
            pltpu.VMEM((WINDOW, KVW), F32),
            pltpu.VMEM((2, chunks, KT, width), F32),
            pltpu.VMEM((2, chunks, KT, width), BF16),
            pltpu.VMEM((4, HDIM, WINDOW), BF16),
            pltpu.VMEM((WINDOW, TILE), F32),
            pltpu.VMEM((units, 2, width, HDIM), BF16),
            pltpu.VMEM((units, 2, HDIM, width), BF16),
            pltpu.SemaphoreType.DMA((20,)),
        ],
        compiler_params=pltpu.CompilerParams(vmem_limit_bytes=28 * 1024 * 1024),
        cost_estimate=pl.CostEstimate(flops=8_000_000_000, bytes_accessed=8_000_000, transcendentals=4_000_000),
        name="attention",
    )(place, queries, out_grad, *received, kv0, kv_b, kv_c, kv_a, docs)


def arrived_kernel(docs_ref, *refs):
    refs[-1][...] = docs_ref[...]


def arrived(docs, received, work):
    return pl.pallas_call(
        arrived_kernel,
        in_specs=[VMEM] + [ANY] * len(received),
        out_specs=VMEM,
        out_shape=struct(docs.shape, docs.dtype),
        compiler_params=SMALL,
        cost_estimate=pl.CostEstimate(flops=work, bytes_accessed=1_000_000, transcendentals=0),
        name="arrived",
    )(docs, *received)


def total_kernel(x_ref, own_ref, b_ref, c_ref, docs_ref, *outs):
    del docs_ref
    for p, out in enumerate(outs):
        rows = pl.ds(pl.multiple_of(lax.rem(x_ref[0] + p, 4) * PART, PART), PART)
        out[...] = (own_ref[rows] + b_ref[rows].astype(F32) + c_ref[rows].astype(F32)).astype(BF16)


def total(place, own, back_b, back_c, docs):
    return pl.pallas_call(
        total_kernel,
        in_specs=[SMEM] + [VMEM] * 4,
        out_specs=[VMEM] * 4,
        out_shape=[struct((PART, KVW), BF16)] * 4,
        compiler_params=SMALL,
        name="total",
    )(place, own, back_b, back_c, docs)


def around(block, distance):
    return lax.ppermute(block, "head", [(i, (i + distance) % 4) for i in range(4)])


def over_chips(block, routes):
    chips = lax.axis_size("chip")
    pairs = [
        (2 * c + k, 2 * (c + step) + to)
        for c in range(chips)
        for k, step, to in routes
        if 0 <= c + step < chips
    ]
    return lax.ppermute(block, ("chip", "core"), pairs)


def local(queries, keys, values, out_grad, doc_ids):
    x = lax.axis_index("head")
    place = jnp.stack([x, lax.axis_index("core")]).astype(jnp.int32)
    doc_number = doc_ids + 1
    docs_low = jnp.pad(doc_number.astype(BF16)[None, :], ((0, 15), (0, KVW - ROWS)))
    docs = jnp.broadcast_to(doc_number.astype(F32)[None, :], (8, ROWS))
    kv_pieces = cut(x, keys, values)
    kv_received = [around(kv_pieces[p], p) for p in (1, 2, 3)]
    q_pieces = pack(place, queries, out_grad)
    kv_received, q_pieces = lax.optimization_barrier((kv_received, q_pieces))
    q_received = [around(piece, p + 1) for p, piece in enumerate(q_pieces)]
    turn = [kv_received[2], kv_received[1], kv_received[0], kv_pieces[0]]
    rows = jnp.stack(turn + turn[:3])
    rows = lax.dynamic_slice_in_dim(rows, 3 - x, 4, 0).reshape(ROWS, KVW)
    kv0 = jnp.concatenate([rows, docs_low], 0)
    kv_c = over_chips(kv0, [(0, 1, 0), (1, 1, 1)])
    kv_b = over_chips(kv0, [(0, 0, 1), (1, 2, 0)])
    kv_c, docs = lax.optimization_barrier((kv_c, arrived(docs, q_received, 40_000_000_000)))
    kv_a = over_chips(kv_c, [(0, 0, 1), (1, 0, 0)])
    o0, o1, o2, o3, own, far, swap, near = attention(
        place, queries, out_grad, q_received, kv0, kv_b, kv_c, kv_a, docs
    )
    back_a = over_chips(swap, [(0, 0, 1), (1, 0, 0)])
    near = (near + back_a.astype(F32)).astype(BF16)
    back_b = over_chips(far, [(1, 0, 0), (0, -2, 1)])
    back_c = over_chips(near, [(0, -1, 0), (1, -1, 1)])
    outs = [o0] + [around(piece, p) for p, piece in ((1, o1), (2, o2), (3, o3))]
    docs = arrived(docs, outs[1:], 4_000_000_000)
    parts = total(place, own, back_b, back_c, docs)
    grads = [parts[0]] + [around(parts[p], p) for p in (1, 2, 3)]
    attention_out, query_grad = unpack(place, outs)
    key_grad, value_grad = unpack(place, grads)
    return attention_out, query_grad, key_grad, value_grad


def solution(mesh):
    chips = mesh.devices.size // 8
    mesh = Mesh(mesh.devices.reshape(chips, 2, 4), ("chip", "core", "head"))
    rows = P(("chip", "core", "head"), None)
    return jax.shard_map(
        local,
        mesh=mesh,
        in_specs=(rows, rows, rows, rows, P(("chip", "core"))),
        out_specs=(rows, rows, rows, rows),
        check_vma=False,
    )
```

```python
import functools
import math

import jax
import jax.numpy as jnp
from jax import lax
from jax.experimental import pallas as pl
from jax.experimental.pallas import tpu as pltpu
from jax.sharding import Mesh, PartitionSpec as P

HDIM = 128
ROWS = 384
PART = 96
KVW = 4 * HDIM
QW = 4 * HDIM
WINDOW = 4 * ROWS
TILE = 128
KT = 256
SPAN = 3 * ROWS + TILE
MASKED = -1e30
SCALE = HDIM**-0.5
EXP_SCALE = SCALE * math.log2(math.e)
SMALL = pltpu.CompilerParams(vmem_limit_bytes=4 * 1024 * 1024)
ANY = pl.BlockSpec(memory_space=pl.ANY)
SMEM = pl.BlockSpec(memory_space=pltpu.SMEM)
HBM = pl.BlockSpec(memory_space=pltpu.HBM)
VMEM = pl.BlockSpec(memory_space=pltpu.VMEM)
BF16, F32 = jnp.bfloat16, jnp.float32


def struct(shape, dtype):
    return jax.ShapeDtypeStruct(shape, dtype)


def run_copies(copies):
    for copy in copies:
        copy.start()
    for copy in copies:
        copy.wait()


def copier(sems):
    count = [0]

    def make(src, dst):
        count[0] += 1
        return pltpu.make_async_copy(src, dst, sems.at[count[0] - 1])

    return make


def pack_kernel(width, x_ref, a_ref, b_ref, *refs):
    outs, sems = refs[:-1], refs[-1]
    make = copier(sems)
    copies = []
    for p in range(1, 4):
        for g in range(2):
            place = pl.multiple_of(lax.rem(x_ref[0] + p, 4) * (2 * width) + g * width, width)
            for n, src in enumerate((a_ref, b_ref)):
                at = pl.ds((2 * g + n) * width, width)
                copies.append(make(src.at[:, pl.ds(place, width)], outs[p - 1].at[:, at]))
    run_copies(copies)


def pack(x, a, b):
    width = a.shape[1] // 8
    return pl.pallas_call(
        functools.partial(pack_kernel, width),
        in_specs=[SMEM, ANY, ANY],
        out_specs=[VMEM] * 3,
        out_shape=[struct((PART, 4 * width), BF16)] * 3,
        scratch_shapes=[pltpu.SemaphoreType.DMA((12,))],
        compiler_params=SMALL,
        name="pack",
    )(x, a, b)


def cut(x, a, b):
    width = a.shape[1] // 8
    pieces = []
    for p in range(4):
        place = (x + p) % 4 * (2 * width)
        cuts = [lax.dynamic_slice_in_dim(src, place + g * width, width, 1) for g in range(2) for src in (a, b)]
        pieces.append(jnp.concatenate(cuts, 1))
    return pieces


def unpack_kernel(width, x_ref, *refs):
    parts, outs, sems = refs[:4], refs[4:-1], refs[-1]
    make = copier(sems)
    copies = []
    for p in range(4):
        for g in range(2):
            place = pl.multiple_of(lax.rem(x_ref[0] + 4 - p, 4) * (2 * width) + g * width, width)
            for n, out in enumerate(outs):
                at = pl.ds((2 * g + n) * width, width)
                copies.append(make(parts[p].at[:, at], out.at[:, pl.ds(place, width)]))
    run_copies(copies)


def unpack(x, parts):
    width = parts[0].shape[1] // 4
    whole = struct((PART, 8 * width), BF16)
    return pl.pallas_call(
        functools.partial(unpack_kernel, width),
        in_specs=[SMEM] + [ANY] * 4,
        out_specs=[VMEM] * 2,
        out_shape=[whole] * 2,
        scratch_shapes=[pltpu.SemaphoreType.DMA((16,))],
        compiler_params=SMALL,
        name="unpack",
    )(x, *parts)


def dot(a, b, contract):
    return lax.dot_general(a, b, ((contract[:1], contract[1:]), ((), ())), preferred_element_type=F32)


def attention_kernel(
    x_ref, q_ref, do_ref, q1, q2, q3, kv0, kv_b, kv_c, kv_a, docs_ref,
    o0, o1, o2, o3, own_ref, far_ref, swap_ref, next_ref,
    kv, docs_kv, qd, out, acc, s_scr, p_scr, kvt, doc_col, qs, qt, sems,
):
    make = copier(sems)
    x, core = x_ref[0], x_ref[1]
    slot_b, slot_a = jnp.where(core == 0, 0, 2), jnp.where(core == 0, 2, 0)
    copies = []
    for ref, slot in ((kv0, 3), (kv_c, 1), (kv_b, slot_b), (kv_a, slot_a)):
        copies.append(make(ref.at[pl.ds(0, ROWS)], kv.at[pl.ds(pl.multiple_of(slot * ROWS, ROWS), ROWS)]))
        copies.append(make(ref.at[pl.ds(ROWS, 16)], docs_kv.at[slot]))
    kv_copies = len(copies)
    rows = pl.ds(pl.multiple_of(x * PART, PART), PART)
    for g in range(2):
        own = pl.multiple_of(x * (2 * QW) + g * QW, QW)
        for n, ref in enumerate((q_ref, do_ref)):
            copies.append(make(ref.at[:, pl.ds(own, QW)], qd.at[rows, pl.ds((2 * g + n) * QW, QW)]))
    for p, ref in enumerate((q1, q2, q3)):
        place = pl.multiple_of(lax.rem(x + 3 - p, 4) * PART, PART)
        copies.append(make(ref, qd.at[pl.ds(place, PART)]))
    for copy in copies:
        copy.start()
    acc[...] = jnp.zeros_like(acc)
    for copy in copies[:kv_copies]:
        copy.wait()

    eye = (
        lax.broadcasted_iota(jnp.int32, (HDIM, HDIM), 0) == lax.broadcasted_iota(jnp.int32, (HDIM, HDIM), 1)
    ).astype(BF16)
    key_docs = jnp.concatenate([docs_kv[s][0:1, 0:ROWS] for s in range(4)], 1)
    row_docs = docs_ref[...]
    doc_col[...] = jnp.transpose(jnp.broadcast_to(key_docs.astype(F32), (TILE, WINDOW)))
    for t in range(WINDOW // KT):
        at = slice(t * KT, (t + 1) * KT)
        for n in range(4):
            kvt[n, :, at] = dot(eye, kv[at, n * HDIM : (n + 1) * HDIM], (1, 1)).astype(BF16)
    for copy in copies[kv_copies:]:
        copy.wait()

    width = 4 * TILE
    chunks = range(SPAN // KT)
    units = range(2 * (ROWS // TILE))
    k_cols = [slice(2 * g * HDIM, (2 * g + 1) * HDIM) for g in range(2)]
    v_cols = [slice((2 * g + 1) * HDIM, (2 * g + 2) * HDIM) for g in range(2)]
    state = [{} for _ in units]

    def keys_of(u, c):
        first = u // 2 * TILE + c * KT
        return slice(first, first + KT)

    def rows_of(u):
        return slice(u // 2 * TILE, (u // 2 + 1) * TILE)

    def head_cols(u, n, r):
        first = (u % 2 * 2 + n) * QW + r * HDIM
        return slice(first, first + HDIM)

    def begin(u):
        q = jnp.concatenate([qd[rows_of(u), head_cols(u, 0, r)] for r in range(4)], 0)
        do = jnp.concatenate([qd[rows_of(u), head_cols(u, 1, r)] for r in range(4)], 0)
        qs[u, 0], qs[u, 1] = q, do
        qt[u, 0] = dot(eye, q, (1, 1)).astype(BF16)
        qt[u, 1] = dot(eye, do, (1, 1)).astype(BF16)
        state[u]["high"] = jnp.full((1, width), MASKED, F32)

    def score(u, c):
        at = keys_of(u, c)
        s = dot(kv[at, k_cols[u % 2]], qt[u, 0], (1, 0))
        docs_row = row_docs[0:1, rows_of(u)]
        allowed = doc_col[at, :] == docs_row
        if (c + 1) * KT > SPAN - TILE:
            key_at = lax.broadcasted_iota(jnp.int32, (KT, TILE), 0) + (u // 2 * TILE + c * KT)
            row_at = lax.broadcasted_iota(jnp.int32, (KT, TILE), 1) + (3 * ROWS + u // 2 * TILE)
            allowed = allowed & (key_at <= row_at)
        s = jnp.concatenate([jnp.where(allowed, s[:, r * TILE : (r + 1) * TILE], MASKED) for r in range(4)], 1)
        s_scr[u % 2, c] = s
        state[u]["high"] = jnp.maximum(state[u]["high"], jnp.max(s, 0, keepdims=True))

    def begin_weigh(u):
        state[u]["shift"] = state[u]["high"] * EXP_SCALE
        state[u]["total"] = jnp.zeros((1, width), F32)
        state[u]["o"] = jnp.zeros((HDIM, width), F32)

    def weigh(u, c):
        e = jnp.exp2(s_scr[u % 2, c] * EXP_SCALE - state[u]["shift"])
        low = e.astype(BF16)
        p_scr[u % 2, c] = low
        state[u]["total"] += jnp.sum(e, 0, keepdims=True)
        state[u]["o"] += dot(kvt[2 * (u % 2) + 1, :, keys_of(u, c)], low, (1, 0))

    def begin_back(u):
        inverse = 1.0 / state[u]["total"]
        o_t = (state[u]["o"] * inverse).astype(BF16).astype(F32)
        state[u]["inverse"] = inverse
        state[u]["dots"] = jnp.sum(qt[u, 1].astype(F32) * o_t, 0, keepdims=True)
        state[u]["dq"] = jnp.zeros((HDIM, width), F32)
        for r in range(4):
            lanes = slice(r * TILE, (r + 1) * TILE)
            out[rows_of(u), head_cols(u, 0, r)] = jnp.transpose(o_t[:, lanes]).astype(BF16)

    def back(u, c):
        at = keys_of(u, c)
        probs = p_scr[u % 2, c].astype(F32) * state[u]["inverse"]
        dp = dot(kv[at, v_cols[u % 2]], qt[u, 1], (1, 0))
        ds = (probs * (dp - state[u]["dots"])).astype(BF16)
        acc[at, v_cols[u % 2]] += dot(probs.astype(BF16), qs[u, 1], (1, 0))
        acc[at, k_cols[u % 2]] += dot(ds, qs[u, 0], (1, 0))
        state[u]["dq"] += dot(kvt[2 * (u % 2), :, at], ds, (1, 0))

    def end_back(u):
        for r in range(4):
            lanes = slice(r * TILE, (r + 1) * TILE)
            out[rows_of(u), head_cols(u, 1, r)] = jnp.transpose(state[u]["dq"][:, lanes] * SCALE).astype(BF16)

    for u in units:
        begin(u)
    for c in chunks:
        score(0, c)
    begin_weigh(0)
    for c in chunks:
        weigh(0, c)
    for u in units:
        begin_back(u)
        later = []
        if u + 1 < len(units):
            later = [functools.partial(score, u + 1, c) for c in chunks]
            later.append(functools.partial(begin_weigh, u + 1))
            later += [functools.partial(weigh, u + 1, c) for c in chunks]
        for c in chunks:
            back(u, c)
            for _ in range(3 if c == 0 else 2):
                if later:
                    later.pop(0)()
        end_back(u)

    copies = []
    for p, ref in enumerate((o0, o1, o2, o3)):
        place = pl.multiple_of(lax.rem(x + p, 4) * PART, PART)
        copies.append(make(out.at[pl.ds(place, PART)], ref))
    for copy in copies:
        copy.start()

    def gradient(slot):
        part = acc[pl.ds(pl.multiple_of(slot * ROWS, ROWS), ROWS), :]
        scales = (SCALE, 1.0, SCALE, 1.0)
        return jnp.concatenate([part[:, n * HDIM : (n + 1) * HDIM] * scales[n] for n in range(4)], 1)

    own_ref[...] = gradient(3).astype(BF16)
    next_ref[...] = gradient(1).astype(BF16)
    far_ref[...] = gradient(slot_b).astype(BF16)
    swap_ref[...] = gradient(slot_a).astype(BF16)
    for copy in copies:
        copy.wait()


def attention(place, queries, out_grad, received, kv0, kv_b, kv_c, kv_a, docs):
    piece = struct((PART, 4 * QW), BF16)
    low_grad = struct((ROWS, KVW), BF16)
    units, chunks, width = 2 * (ROWS // TILE), SPAN // KT, 4 * TILE
    return pl.pallas_call(
        attention_kernel,
        in_specs=[SMEM] + [ANY] * 9 + [VMEM],
        out_specs=[ANY] * 4 + [VMEM] * 4,
        out_shape=[piece] * 4 + [low_grad] * 4,
        scratch_shapes=[
            pltpu.VMEM((WINDOW, KVW), BF16),
            pltpu.VMEM((4, 16, KVW), BF16),
            pltpu.VMEM((ROWS, 4 * QW), BF16),
            pltpu.VMEM((ROWS, 4 * QW), BF16),
            pltpu.VMEM((WINDOW, KVW), F32),
            pltpu.VMEM((2, chunks, KT, width), F32),
            pltpu.VMEM((2, chunks, KT, width), BF16),
            pltpu.VMEM((4, HDIM, WINDOW), BF16),
            pltpu.VMEM((WINDOW, TILE), F32),
            pltpu.VMEM((units, 2, width, HDIM), BF16),
            pltpu.VMEM((units, 2, HDIM, width), BF16),
            pltpu.SemaphoreType.DMA((20,)),
        ],
        compiler_params=pltpu.CompilerParams(vmem_limit_bytes=28 * 1024 * 1024),
        cost_estimate=pl.CostEstimate(flops=8_000_000_000, bytes_accessed=8_000_000, transcendentals=4_000_000),
        name="attention",
    )(place, queries, out_grad, *received, kv0, kv_b, kv_c, kv_a, docs)


def arrived_kernel(docs_ref, *refs):
    refs[-1][...] = docs_ref[...]


def arrived(docs, received, work):
    return pl.pallas_call(
        arrived_kernel,
        in_specs=[VMEM] + [ANY] * len(received),
        out_specs=VMEM,
        out_shape=struct(docs.shape, docs.dtype),
        compiler_params=SMALL,
        cost_estimate=pl.CostEstimate(flops=work, bytes_accessed=1_000_000, transcendentals=0),
        name="arrived",
    )(docs, *received)


def total_kernel(x_ref, own_ref, b_ref, c_ref, docs_ref, *outs):
    del docs_ref
    for p, out in enumerate(outs):
        rows = pl.ds(pl.multiple_of(lax.rem(x_ref[0] + p, 4) * PART, PART), PART)
        out[...] = (own_ref[rows].astype(F32) + b_ref[rows].astype(F32) + c_ref[rows].astype(F32)).astype(BF16)


def total(place, own, back_b, back_c, docs):
    return pl.pallas_call(
        total_kernel,
        in_specs=[SMEM] + [VMEM] * 4,
        out_specs=[VMEM] * 4,
        out_shape=[struct((PART, KVW), BF16)] * 4,
        compiler_params=SMALL,
        name="total",
    )(place, own, back_b, back_c, docs)


def around(block, distance):
    return lax.ppermute(block, "head", [(i, (i + distance) % 4) for i in range(4)])


def over_chips(block, routes):
    chips = lax.axis_size("chip")
    pairs = [
        (2 * c + k, 2 * (c + step) + to)
        for c in range(chips)
        for k, step, to in routes
        if 0 <= c + step < chips
    ]
    return lax.ppermute(block, ("chip", "core"), pairs)


def local(queries, keys, values, out_grad, doc_ids):
    x = lax.axis_index("head")
    place = jnp.stack([x, lax.axis_index("core")]).astype(jnp.int32)
    doc_number = doc_ids + 1
    docs_low = jnp.pad(doc_number.astype(BF16)[None, :], ((0, 15), (0, KVW - ROWS)))
    docs = jnp.broadcast_to(doc_number.astype(F32)[None, :], (8, ROWS))
    kv_pieces = cut(x, keys, values)
    kv_received = [around(kv_pieces[p], p) for p in (1, 2, 3)]
    q_pieces = pack(place, queries, out_grad)
    kv_received, q_pieces = lax.optimization_barrier((kv_received, q_pieces))
    q_received = [around(piece, p + 1) for p, piece in enumerate(q_pieces)]
    turn = [kv_received[2], kv_received[1], kv_received[0], kv_pieces[0]]
    rows = jnp.stack(turn + turn[:3])
    rows = lax.dynamic_slice_in_dim(rows, 3 - x, 4, 0).reshape(ROWS, KVW)
    kv0 = jnp.concatenate([rows, docs_low], 0)
    kv_c = over_chips(kv0, [(0, 1, 0), (1, 1, 1)])
    kv_b = over_chips(kv0, [(0, 0, 1), (1, 2, 0)])
    kv_c, docs = lax.optimization_barrier((kv_c, arrived(docs, q_received, 40_000_000_000)))
    kv_a = over_chips(kv_c, [(0, 0, 1), (1, 0, 0)])
    o0, o1, o2, o3, own, far, swap, near = attention(
        place, queries, out_grad, q_received, kv0, kv_b, kv_c, kv_a, docs
    )
    back_a = over_chips(swap, [(0, 0, 1), (1, 0, 0)])
    near = (near.astype(F32) + back_a.astype(F32)).astype(BF16)
    back_b = over_chips(far, [(1, 0, 0), (0, -2, 1)])
    back_c = over_chips(near, [(0, -1, 0), (1, -1, 1)])
    outs = [o0] + [around(piece, p) for p, piece in ((1, o1), (2, o2), (3, o3))]
    docs = arrived(docs, outs[1:], 4_000_000_000)
    parts = total(place, own, back_b, back_c, docs)
    grads = [parts[0]] + [around(parts[p], p) for p in (1, 2, 3)]
    attention_out, query_grad = unpack(place, outs)
    key_grad, value_grad = unpack(place, grads)
    return attention_out, query_grad, key_grad, value_grad


def solution(mesh):
    chips = mesh.devices.size // 8
    mesh = Mesh(mesh.devices.reshape(chips, 2, 4), ("chip", "core", "head"))
    rows = P(("chip", "core", "head"), None)
    return jax.shard_map(
        local,
        mesh=mesh,
        in_specs=(rows, rows, rows, rows, P(("chip", "core"))),
        out_specs=(rows, rows, rows, rows),
        check_vma=False,
    )
```
